256 devices in a mesh: grp: 16 (over y, x), seq: 16 (over z, core).
Axes of the slice: x: 4, y: 4, z: 8, core: 2. Of those that a mesh axis runs over, the one named last changes fastest.
Arguments:
- queries: bfloat16 [16, 16, 512, 1536], P('grp', 'seq'), may hold values from -5 to 5
- keys: bfloat16 [16, 16, 512, 1536], P('grp', 'seq'), may hold values from -5 to 5
- values: bfloat16 [16, 16, 512, 1536], P('grp', 'seq'), may hold values from -5 to 5
- clip_frames: int32 [8, 4], replicated, may hold values from 1 to 8, 16 in all within a row
- clip_pixels: int32 [8, 4], replicated, may hold values from 256 to 1024
Outputs:
- attended: bfloat16 [16, 16, 512, 1536], P('grp', 'seq')
The draws below stay inside these ranges and needn't reach their ends.
All inputs are finite; a program needn't handle non-finite values.
Results may differ from the reference program's by a relative error of at most 0.0051.
Values may be sent and summed in bfloat16 or wider, within the bound.
No kernel may reach another device: no remote copies, remote signals or barrier semaphores. Data moves between devices by JAX's collectives and lax.ppermute only.
A program may use at most 192 MiB of HBM per device.

```python
import math
import jax
import jax.numpy as jnp
import numpy as np
from jax import lax

H = 12
DH = 128
S_HALF = 512
CLIPS = 4
HD = 1536
S = 1024
FRAMES = 16
GROUPS = 8
N_GRP = 16


def draw_queries(key, part):
    key = jax.random.fold_in(key, 1)
    shape = (N_GRP, FRAMES, S_HALF, HD)
    drawn = jax.random.truncated_normal(key, -5.0, 5.0, shape, jnp.float32)
    return drawn.astype(jnp.bfloat16)


def draw_keys(key, part):
    key = jax.random.fold_in(key, 2)
    shape = (N_GRP, FRAMES, S_HALF, HD)
    drawn = jax.random.truncated_normal(key, -5.0, 5.0, shape, jnp.float32)
    return drawn.astype(jnp.bfloat16)


def with_ends(values, stream_key, least, largest):
    longest = values.shape.index(max(values.shape))
    spots = []
    for shift in (0, 1):
        where = [jax.random.randint(jax.random.fold_in(stream_key, axis), (), 0, length) for axis, length in enumerate(values.shape)]
        where[longest] = (where[longest] + shift) % values.shape[longest]
        spots.append(tuple(where))
    return values.at[spots[0]].set(least).at[spots[1]].set(largest)


def level_of(key, shape, cuts, least, largest):
    loudness = 1.0
    for position, blocks in cuts:
        steps = jax.random.uniform(jax.random.fold_in(jax.random.fold_in(key, 6), position), (blocks,), jnp.float32, least / len(cuts), largest / len(cuts))
        loudness = loudness * jnp.repeat(jnp.exp(steps), shape[position] // blocks).reshape((-1,) + (1,) * (len(shape) - 1 - position))
    return loudness


def length_profile(amount, total, most, lean):
    loads = [(1 << 20) // math.isqrt(grade ** lean) + 1 for grade in range(2, amount + 1)]
    spare, given = total - most - (amount - 1), [1] * (amount - 1)
    while spare > 0:
        candidates = [i for i in range(amount - 1) if given[i] < most]
        mass, left = sum([loads[i] for i in candidates]), spare
        for i in candidates:
            extra = min(most - given[i], max(1, left * loads[i] // mass), spare)
            given[i] = given[i] + extra
            spare = spare - extra
    return np.array([most] + given)


def ragged(rng, number_of, total, bound, slope):
    if number_of == 2:
        one = jax.random.randint(rng, (), max(1, total - bound), min(bound, total - 1) + 1)
        return jnp.stack([one, total - one])
    lengths = jnp.asarray(length_profile(number_of, total, bound, slope), jnp.int32)
    pairs = (number_of - 1) // 2
    source_of, taker = lengths[1:1 + 2 * pairs:2], lengths[2:2 + 2 * pairs:2]
    slack = jnp.minimum(source_of - 1, bound - taker)
    shifted = jax.random.randint(jax.random.fold_in(rng, 1), (pairs,), 0, 1 << 20) % (slack + 1)
    lengths = lengths.at[1:1 + 2 * pairs:2].set(source_of - shifted).at[2:2 + 2 * pairs:2].set(taker + shifted)
    return lengths[jax.random.permutation(jax.random.fold_in(rng, 2), number_of)]


def normal_values(own_key, dims, deviation, most, split=(), held_as=jnp.bfloat16):
    array = deviation * jax.random.normal(own_key, dims, jnp.float32)
    if split:
        array = array * level_of(own_key, dims, split, -0.22, 0.18)
    return jnp.clip(array, -most, most).astype(held_as)


def setup_inputs(seed: int = 0) -> dict:
    splits = jax.random.split(jax.random.key(seed), 6)
    queries = draw_queries(jax.random.fold_in(splits[5], 71), 0)
    keys = draw_keys(jax.random.fold_in(splits[5], 71), 0)
    values = normal_values(splits[2], (N_GRP, FRAMES, S_HALF, HD), 1.0, 5.0, ((0, 16), (1, 16)))
    clip_frames = jax.vmap(lambda own: ragged(own, CLIPS, FRAMES, FRAMES // 2, 1))(jax.random.split(splits[3], GROUPS)).reshape((GROUPS, CLIPS)).astype(jnp.int32)
    clip_pixels = with_ends(jax.random.randint(splits[4], (GROUPS, CLIPS), S // 4, S + 1), jax.random.fold_in(splits[4], 1), S // 4, S).astype(jnp.int32)
    return dict(queries=queries, keys=keys, values=values, clip_frames=clip_frames, clip_pixels=clip_pixels)


masked_score = -1e30


def clip_tables(frames_row, pixels_row, total_frames):
    clip_ends = jnp.cumsum(frames_row).astype(jnp.int32)
    frame_ids = jnp.arange(total_frames, dtype=jnp.int32)
    segment = jnp.sum((frame_ids[:, None] >= clip_ends[None, :]).astype(jnp.int32), axis=1)
    member = segment[:, None] == jnp.arange(CLIPS, dtype=jnp.int32)[None, :]
    limits = jnp.sum(jnp.where(member, pixels_row[None, :], 0), axis=1).astype(jnp.int32)
    return segment, limits


def reference(queries, keys, values, clip_frames, clip_pixels):
    factor = DH ** -0.5
    positions = jnp.arange(S, dtype=jnp.int32)

    def whole(tensor):
        return jnp.transpose(tensor, (1, 0, 2, 3)).reshape(FRAMES, S, H, DH)

    def one_frame(blocks):
        q_frame, k_frame, v_frame, limit = blocks
        scores = jnp.einsum("qhd,khd->hqk", q_frame.astype(jnp.float32), k_frame.astype(jnp.float32)) * factor
        scores = jnp.where((positions < limit)[None, None, :], scores, masked_score)
        top_score = jnp.max(scores, axis=-1, keepdims=True)
        weights = jnp.exp(scores - top_score)
        totals = jnp.sum(weights, axis=-1)
        rounded = weights.astype(jnp.bfloat16)
        summed = jnp.einsum("hqk,khd->qhd", rounded.astype(jnp.float32), v_frame.astype(jnp.float32))
        return summed / jnp.transpose(totals)[:, :, None]

    def one_group(inputs):
        q_group, k_group, v_group, frames_row, pixels_row = inputs
        segment, limits = clip_tables(frames_row, pixels_row, FRAMES)
        q_all = whole(q_group)
        k_all = whole(k_group)
        v_all = whole(v_group)
        spatial = lax.map(one_frame, (q_all, k_all, v_all, limits))
        scores = jnp.einsum("fphd,gphd->hpfg", q_all.astype(jnp.float32), k_all.astype(jnp.float32)) * factor
        same_clip = segment[:, None] == segment[None, :]
        scores = jnp.where(same_clip[None, None], scores, masked_score)
        top_score = jnp.max(scores, axis=-1, keepdims=True)
        weights = jnp.exp(scores - top_score)
        totals = jnp.sum(weights, axis=-1)
        rounded = weights.astype(jnp.bfloat16)
        summed = jnp.einsum("hpfg,gphd->fphd", rounded.astype(jnp.float32), v_all.astype(jnp.float32))
        temporal = (summed / jnp.transpose(totals, (2, 1, 0))[..., None]).astype(jnp.bfloat16)
        attended = (spatial + temporal.astype(jnp.float32)).astype(jnp.bfloat16)
        attended = attended.reshape(FRAMES, 2, S_HALF, H * DH)
        return jnp.transpose(attended, (1, 0, 2, 3))

    q_grouped = queries.reshape(GROUPS, 2, FRAMES, S_HALF, H * DH)
    k_grouped = keys.reshape(GROUPS, 2, FRAMES, S_HALF, H * DH)
    v_grouped = values.reshape(GROUPS, 2, FRAMES, S_HALF, H * DH)
    result = lax.map(one_group, (q_grouped, k_grouped, v_grouped, clip_frames, clip_pixels))
    return result.reshape(N_GRP, FRAMES, S_HALF, H * DH)
```

```python
import functools

import jax
import jax.numpy as jnp
from jax import lax
from jax.experimental import pallas as pl
from jax.experimental.pallas import tpu as pltpu
from jax.sharding import PartitionSpec as P

DH = 128
CLIPS = 4
MASKED = -1e30
SCALE = DH**-0.5 * 1.4426950408889634
TBLOCK = 16
VMEM_LIMIT = 40 * 1024 * 1024


def scores_of(a, b):
    return lax.dot_general(a, b, (((1,), (1,)), ((), ())), preferred_element_type=jnp.float32)


def spatial_kernel(cf_ref, cp_ref, q_ref, k_ref, v_ref, fk_ref, fv_ref, o_ref):
    group_slot = lax.axis_index("grp")
    frame = lax.axis_index("seq")
    group = group_slot // 2
    half = group_slot % 2
    rows = q_ref.shape[0]
    limit = cp_ref[group, 0]
    end = cf_ref[group, 0]
    for clip in range(1, CLIPS):
        limit = jnp.where(frame >= end, cp_ref[group, clip], limit)
        end = end + cf_ref[group, clip]
    column = lax.broadcasted_iota(jnp.int32, (1, rows), 1)
    own_keep = column < limit - half * rows
    far_keep = column < limit - (1 - half) * rows
    for head in range(q_ref.shape[1] // DH):
        lanes = pl.ds(head * DH, DH)
        q = q_ref[:, lanes]
        own = jnp.where(own_keep, scores_of(q, k_ref[:, lanes]), MASKED)
        far = jnp.where(far_keep, scores_of(q, fk_ref[:, lanes]), MASKED)
        top = jnp.maximum(
            jnp.max(own, axis=1, keepdims=True), jnp.max(far, axis=1, keepdims=True)
        )
        own = jnp.exp2((own - top) * SCALE)
        far = jnp.exp2((far - top) * SCALE)
        total = jnp.sum(own, axis=1, keepdims=True) + jnp.sum(far, axis=1, keepdims=True)
        summed = jnp.dot(
            own.astype(jnp.bfloat16), v_ref[:, lanes], preferred_element_type=jnp.float32
        ) + jnp.dot(
            far.astype(jnp.bfloat16), fv_ref[:, lanes], preferred_element_type=jnp.float32
        )
        o_ref[:, lanes] = summed / total


def spatial_attention(clip_frames, clip_pixels, q, k, v, far_k, far_v):
    rows, width = q.shape
    heads = width // DH
    block = pl.BlockSpec((rows, DH), lambda h: (0, h))
    table = pl.BlockSpec(memory_space=pltpu.SMEM)
    return pl.pallas_call(
        spatial_kernel,
        grid=(heads,),
        in_specs=[table, table] + [block] * 5,
        out_specs=block,
        out_shape=jax.ShapeDtypeStruct((rows, width), jnp.float32),
        compiler_params=pltpu.CompilerParams(vmem_limit_bytes=VMEM_LIMIT),
        cost_estimate=pl.CostEstimate(
            flops=8 * rows * rows * width,
            bytes_accessed=rows * width * 14,
            transcendentals=2 * rows * rows * heads,
        ),
        name="spatial",
    )(clip_frames, clip_pixels, q, k, v, far_k, far_v)


def segment_of(frame, ends):
    return sum((frame >= end).astype(jnp.int32) for end in ends)


def temporal_kernel(cf_ref, qkv_ref, o_ref, keep_ref):
    frames, rows = o_ref.shape[0], o_ref.shape[1]
    size = frames * TBLOCK
    group = lax.axis_index("grp") // 2

    @pl.when(pl.program_id(0) == 0)
    def _():
        ends = []
        end = 0
        for clip in range(CLIPS):
            end = end + cf_ref[group, clip]
            ends.append(end)
        row = lax.broadcasted_iota(jnp.int32, (size, size), 0)
        col = lax.broadcasted_iota(jnp.int32, (size, size), 1)
        same_clip = segment_of(row // TBLOCK, ends) == segment_of(col // TBLOCK, ends)
        same_spot = row % TBLOCK == col % TBLOCK
        keep_ref[...] = jnp.where(same_clip & same_spot, 1.0, 0.0)

    keep = keep_ref[...] > 0.5
    for block in range(rows // TBLOCK):

        def part(which):
            at = pl.ds(which * rows + block * TBLOCK, TBLOCK)
            return qkv_ref[:, at, :].reshape(size, DH)

        scores = jnp.where(keep, scores_of(part(0), part(1)), MASKED)
        top = jnp.max(scores, axis=1, keepdims=True)
        weights = jnp.exp2((scores - top) * SCALE)
        total = jnp.sum(weights, axis=1, keepdims=True)
        summed = jnp.dot(weights.astype(jnp.bfloat16), part(2), preferred_element_type=jnp.float32)
        out = (summed / total).astype(o_ref.dtype)
        o_ref[:, pl.ds(block * TBLOCK, TBLOCK), :] = out.reshape(frames, TBLOCK, DH)


def temporal_attention(clip_frames, qkv):
    frames, rows3, width = qkv.shape
    rows = rows3 // 3
    heads = width // DH
    size = frames * TBLOCK
    return pl.pallas_call(
        temporal_kernel,
        grid=(heads,),
        in_specs=[
            pl.BlockSpec(memory_space=pltpu.SMEM),
            pl.BlockSpec((frames, rows3, DH), lambda h: (0, 0, h)),
        ],
        out_specs=pl.BlockSpec((frames, rows, DH), lambda h: (0, 0, h)),
        out_shape=jax.ShapeDtypeStruct((frames, rows, width), jnp.bfloat16),
        scratch_shapes=[pltpu.VMEM((size, size), jnp.float32)],
        compiler_params=pltpu.CompilerParams(vmem_limit_bytes=VMEM_LIMIT),
        cost_estimate=pl.CostEstimate(
            flops=4 * size * size * width * rows // TBLOCK,
            bytes_accessed=frames * rows * width * 8,
            transcendentals=size * size * heads * rows // TBLOCK,
        ),
        name="temporal",
    )(clip_frames, qkv)


def on_device(queries, keys, values, clip_frames, clip_pixels):
    rows, width = queries.shape[2], queries.shape[3]
    frames = lax.axis_size("seq")
    share = rows // frames
    q, k, v = queries[0, 0], keys[0, 0], values[0, 0]
    swap = [(i, i ^ 1) for i in range(lax.axis_size("grp"))]
    far_k = lax.ppermute(k, "grp", swap)
    far_v = lax.ppermute(v, "grp", swap)
    qkv = jnp.concatenate([x.reshape(frames, share, width) for x in (q, k, v)], axis=1)
    moved = lax.all_to_all(qkv, "seq", split_axis=0, concat_axis=0, tiled=True)
    temporal = temporal_attention(clip_frames, moved)
    spatial = spatial_attention(clip_frames, clip_pixels, q, k, v, far_k, far_v)
    back = lax.all_to_all(temporal, "seq", split_axis=0, concat_axis=0, tiled=True)
    attended = spatial + back.reshape(rows, width).astype(jnp.float32)
    return attended.astype(jnp.bfloat16)[None, None]


def solution(mesh):
    spec = P("grp", "seq", None, None)
    return jax.shard_map(
        on_device, mesh=mesh, in_specs=(spec, spec, spec, P(), P()), out_specs=spec, check_vma=False
    )
```

```python
import jax
import jax.numpy as jnp
from jax import lax
from jax.experimental import pallas as pl
from jax.experimental.pallas import tpu as pltpu
from jax.sharding import PartitionSpec as P

DH = 128
CLIPS = 4
MASKED = -1e30
SCALE = DH**-0.5 * 1.4426950408889634
TBLOCK = 16
PARAMS = pltpu.CompilerParams(vmem_limit_bytes=24 * 1024 * 1024)
SMEM = pl.BlockSpec(memory_space=pltpu.SMEM)


def scores_of(a, b):
    return lax.dot_general(a, b, (((1,), (1,)), ((), ())), preferred_element_type=jnp.float32)


def product(a, b):
    return jnp.dot(a, b, preferred_element_type=jnp.float32)


def spatial_kernel(cf_ref, cp_ref, q_ref, k_ref, v_ref, fk_ref, fv_ref, o_ref):
    group_slot = lax.axis_index("grp")
    frame = lax.axis_index("seq")
    group = group_slot // 2
    half = group_slot % 2
    rows = q_ref.shape[0]
    limit = cp_ref[group, 0]
    end = cf_ref[group, 0]
    for clip in range(1, CLIPS):
        limit = jnp.where(frame >= end, cp_ref[group, clip], limit)
        end = end + cf_ref[group, clip]
    column = lax.broadcasted_iota(jnp.int32, (1, rows), 1)
    own_keep = column < limit - half * rows
    far_keep = column < limit - (1 - half) * rows
    for head in range(q_ref.shape[1] // DH):
        lanes = pl.ds(head * DH, DH)
        q = q_ref[:, lanes]
        own = jnp.where(own_keep, scores_of(q, k_ref[:, lanes]), MASKED)
        far = jnp.where(far_keep, scores_of(q, fk_ref[:, lanes]), MASKED)
        top = jnp.maximum(
            jnp.max(own, axis=1, keepdims=True), jnp.max(far, axis=1, keepdims=True)
        )
        own = jnp.exp2((own - top) * SCALE)
        far = jnp.exp2((far - top) * SCALE)
        total = jnp.sum(own, axis=1, keepdims=True) + jnp.sum(far, axis=1, keepdims=True)
        summed = product(own.astype(jnp.bfloat16), v_ref[:, lanes])
        summed = summed + product(far.astype(jnp.bfloat16), fv_ref[:, lanes])
        o_ref[:, lanes] = summed / total


def spatial_attention(clip_frames, clip_pixels, q, k, v, far_k, far_v, start):
    rows, width = far_k.shape
    heads = width // DH
    block = pl.BlockSpec((rows, DH), lambda h: (0, h))
    whole = pl.BlockSpec((rows, DH), lambda h: (0, h + start // DH))
    return pl.pallas_call(
        spatial_kernel,
        grid=(heads,),
        in_specs=[SMEM, SMEM, whole, whole, whole, block, block],
        out_specs=block,
        out_shape=jax.ShapeDtypeStruct((rows, width), jnp.float32),
        compiler_params=PARAMS,
        cost_estimate=pl.CostEstimate(
            flops=8 * rows * rows * width,
            bytes_accessed=rows * width * 14,
            transcendentals=2 * rows * rows * heads,
        ),
        name="spatial",
    )(clip_frames, clip_pixels, q, k, v, far_k, far_v)


def clip_mask(cf_ref, keep_ref, frames, rolled):
    size = keep_ref.shape[0]
    group = lax.axis_index("grp") // 2
    me = lax.axis_index("seq")
    row = lax.broadcasted_iota(jnp.int32, (size, size), 0)
    col = lax.broadcasted_iota(jnp.int32, (size, size), 1)
    same_spot = row % TBLOCK == col % TBLOCK

    def frame_of(index):
        slot = index // TBLOCK
        if not rolled:
            return slot
        return (me + frames - slot) % frames

    def segment_of(index):
        frame = frame_of(index)
        end = 0
        segment = jnp.zeros_like(frame)
        for clip in range(CLIPS):
            end = end + cf_ref[group, clip]
            segment = segment + (frame >= end).astype(jnp.int32)
        return segment

    keep = same_spot & (segment_of(row) == segment_of(col))
    keep_ref[...] = jnp.where(keep, 0.0, MASKED)


def temporal_block(bias, q, k, v):
    scores = scores_of(q, k) + bias
    top = jnp.max(scores, axis=1, keepdims=True)
    weights = jnp.exp2((scores - top) * SCALE)
    total = jnp.sum(weights, axis=1, keepdims=True)
    return (product(weights.astype(jnp.bfloat16), v) / total).astype(jnp.bfloat16)


def temporal_kernel(cf_ref, qkv_ref, o_ref, keep_ref):
    frames, rows, width = o_ref.shape
    size = frames * TBLOCK

    @pl.when(pl.program_id(0) == 0)
    def _():
        clip_mask(cf_ref, keep_ref, frames, False)

    bias = keep_ref[...]
    for head in range(width // DH):
        lanes = pl.ds(head * DH, DH)
        for block in range(rows // TBLOCK):
            q, k, v = (
                qkv_ref[:, pl.ds(which * rows + block * TBLOCK, TBLOCK), lanes].reshape(size, DH)
                for which in range(3)
            )
            out = temporal_block(bias, q, k, v)
            o_ref[:, pl.ds(block * TBLOCK, TBLOCK), lanes] = out.reshape(frames, TBLOCK, DH)


def temporal_cost(frames, rows, width):
    size = frames * TBLOCK
    return pl.CostEstimate(
        flops=4 * size * size * width * rows // TBLOCK,
        bytes_accessed=frames * rows * width * 8,
        transcendentals=size * size * (width // DH) * rows // TBLOCK,
    )


def temporal_attention(clip_frames, qkv, heads_step):
    frames, rows3, width = qkv.shape
    rows = rows3 // 3
    lanes = heads_step * DH
    size = frames * TBLOCK
    return pl.pallas_call(
        temporal_kernel,
        grid=(width // lanes,),
        in_specs=[SMEM, pl.BlockSpec((frames, rows3, lanes), lambda h: (0, 0, h))],
        out_specs=pl.BlockSpec((frames, rows, lanes), lambda h: (0, 0, h)),
        out_shape=jax.ShapeDtypeStruct((frames, rows, width), jnp.bfloat16),
        scratch_shapes=[pltpu.VMEM((size, size), jnp.float32)],
        compiler_params=PARAMS,
        cost_estimate=temporal_cost(frames, rows, width),
        name="temporal",
    )(clip_frames, qkv)


def all_to_all(array):
    return lax.all_to_all(array, "seq", split_axis=0, concat_axis=0, tiled=True)


def on_device(queries, keys, values, clip_frames, clip_pixels):
    rows, width = queries.shape[2], queries.shape[3]
    frames = lax.axis_size("seq")
    q, k, v = queries[0, 0], keys[0, 0], values[0, 0]
    swap = [(i, i ^ 1) for i in range(lax.axis_size("grp"))]
    packed = jnp.concatenate([x.reshape(frames, rows // frames, width) for x in (q, k, v)], axis=1)
    moved = all_to_all(packed)
    far_k = lax.ppermute(k, "grp", swap)
    far_v = lax.ppermute(v, "grp", swap)
    spatial = spatial_attention(clip_frames, clip_pixels, q, k, v, far_k, far_v, 0)
    moved, spatial = lax.optimization_barrier((moved, spatial))
    back = all_to_all(temporal_attention(clip_frames, moved, 4))
    attended = spatial + back.reshape(rows, width).astype(jnp.float32)
    return attended.astype(jnp.bfloat16)[None, None]


def solution(mesh):
    spec = P("grp", "seq", None, None)
    return jax.shard_map(
        on_device, mesh=mesh, in_specs=(spec, spec, spec, P(), P()), out_specs=spec, check_vma=False
    )
```

```python
import jax
import jax.numpy as jnp
from jax import lax
from jax.experimental import pallas as pl
from jax.experimental.pallas import tpu as pltpu
from jax.sharding import PartitionSpec as P

DH = 128
CLIPS = 4
MASKED = -1e30
SCALE = DH**-0.5 * 1.4426950408889634
TBLOCK = 16
PARAMS = pltpu.CompilerParams(vmem_limit_bytes=24 * 1024 * 1024)
SMEM = pl.BlockSpec(memory_space=pltpu.SMEM)


def scores_of(a, b):
    return lax.dot_general(a, b, (((1,), (1,)), ((), ())), preferred_element_type=jnp.float32)


def product(a, b):
    return jnp.dot(a, b, preferred_element_type=jnp.float32)


def spatial_kernel(cf_ref, cp_ref, q_ref, k_ref, v_ref, fk_ref, fv_ref, o_ref):
    group_slot = lax.axis_index("grp")
    frame = lax.axis_index("seq")
    group = group_slot // 2
    half = group_slot % 2
    rows = q_ref.shape[0]
    limit = cp_ref[group, 0]
    end = cf_ref[group, 0]
    for clip in range(1, CLIPS):
        limit = jnp.where(frame >= end, cp_ref[group, clip], limit)
        end = end + cf_ref[group, clip]
    column = lax.broadcasted_iota(jnp.int32, (1, rows), 1)
    own_keep = column < limit - half * rows
    far_keep = column < limit - (1 - half) * rows
    for head in range(q_ref.shape[1] // DH):
        lanes = pl.ds(head * DH, DH)
        q = q_ref[:, lanes]
        own = jnp.where(own_keep, scores_of(q, k_ref[:, lanes]), MASKED)
        far = jnp.where(far_keep, scores_of(q, fk_ref[:, lanes]), MASKED)
        top = jnp.maximum(
            jnp.max(own, axis=1, keepdims=True), jnp.max(far, axis=1, keepdims=True)
        )
        own = jnp.exp2((own - top) * SCALE)
        far = jnp.exp2((far - top) * SCALE)
        total = jnp.sum(own, axis=1, keepdims=True) + jnp.sum(far, axis=1, keepdims=True)
        summed = product(own.astype(jnp.bfloat16), v_ref[:, lanes])
        summed = summed + product(far.astype(jnp.bfloat16), fv_ref[:, lanes])
        o_ref[:, lanes] = summed / total


def spatial_attention(clip_frames, clip_pixels, q, k, v, far_k, far_v, start):
    rows, width = far_k.shape
    heads = width // DH
    block = pl.BlockSpec((rows, DH), lambda h: (0, h))
    whole = pl.BlockSpec((rows, DH), lambda h: (0, h + start // DH))
    return pl.pallas_call(
        spatial_kernel,
        grid=(heads,),
        in_specs=[SMEM, SMEM, whole, whole, whole, block, block],
        out_specs=block,
        out_shape=jax.ShapeDtypeStruct((rows, width), jnp.float32),
        compiler_params=PARAMS,
        cost_estimate=pl.CostEstimate(
            flops=8 * rows * rows * width,
            bytes_accessed=rows * width * 14,
            transcendentals=2 * rows * rows * heads,
        ),
        name="spatial",
    )(clip_frames, clip_pixels, q, k, v, far_k, far_v)


def clip_mask(cf_ref, keep_ref, frames, rolled):
    size = keep_ref.shape[0]
    group = lax.axis_index("grp") // 2
    me = lax.axis_index("seq")
    row = lax.broadcasted_iota(jnp.int32, (size, size), 0)
    col = lax.broadcasted_iota(jnp.int32, (size, size), 1)
    same_spot = row % TBLOCK == col % TBLOCK

    def frame_of(index):
        slot = index // TBLOCK
        if not rolled:
            return slot
        return (me + frames - slot) % frames

    def segment_of(index):
        frame = frame_of(index)
        end = 0
        segment = jnp.zeros_like(frame)
        for clip in range(CLIPS):
            end = end + cf_ref[group, clip]
            segment = segment + (frame >= end).astype(jnp.int32)
        return segment

    keep = same_spot & (segment_of(row) == segment_of(col))
    keep_ref[...] = jnp.where(keep, 0.0, MASKED)


def temporal_block(bias, q, k, v):
    scores = scores_of(q, k) + bias
    top = jnp.max(scores, axis=1, keepdims=True)
    weights = jnp.exp2((scores - top) * SCALE).astype(jnp.bfloat16)
    summed = product(weights, jnp.concatenate([v, jnp.ones_like(v)], axis=1))
    return (summed[:, :DH] / summed[:, DH:]).astype(jnp.bfloat16)


def temporal_kernel(cf_ref, qkv_ref, o_ref, keep_ref):
    frames, rows, width = o_ref.shape
    size = frames * TBLOCK

    @pl.when(pl.program_id(0) == 0)
    def _():
        clip_mask(cf_ref, keep_ref, frames, False)

    bias = keep_ref[...]
    for head in range(width // DH):
        lanes = pl.ds(head * DH, DH)
        for block in range(rows // TBLOCK):
            q, k, v = (
                qkv_ref[:, pl.ds(which * rows + block * TBLOCK, TBLOCK), lanes].reshape(size, DH)
                for which in range(3)
            )
            out = temporal_block(bias, q, k, v)
            o_ref[:, pl.ds(block * TBLOCK, TBLOCK), lanes] = out.reshape(frames, TBLOCK, DH)


def temporal_cost(frames, rows, width):
    size = frames * TBLOCK
    return pl.CostEstimate(
        flops=4 * size * size * width * rows // TBLOCK,
        bytes_accessed=frames * rows * width * 8,
        transcendentals=size * size * (width // DH) * rows // TBLOCK,
    )


def temporal_attention(clip_frames, qkv, heads_step):
    frames, rows3, width = qkv.shape
    rows = rows3 // 3
    lanes = heads_step * DH
    size = frames * TBLOCK
    return pl.pallas_call(
        temporal_kernel,
        grid=(width // lanes,),
        in_specs=[SMEM, pl.BlockSpec((frames, rows3, lanes), lambda h: (0, 0, h))],
        out_specs=pl.BlockSpec((frames, rows, lanes), lambda h: (0, 0, h)),
        out_shape=jax.ShapeDtypeStruct((frames, rows, width), jnp.bfloat16),
        scratch_shapes=[pltpu.VMEM((size, size), jnp.float32)],
        compiler_params=PARAMS,
        cost_estimate=temporal_cost(frames, rows, width),
        name="temporal",
    )(clip_frames, qkv)


def all_to_all(array):
    return lax.all_to_all(array, "seq", split_axis=0, concat_axis=0, tiled=True)


def on_device(queries, keys, values, clip_frames, clip_pixels):
    rows, width = queries.shape[2], queries.shape[3]
    frames = lax.axis_size("seq")
    q, k, v = queries[0, 0], keys[0, 0], values[0, 0]
    swap = [(i, i ^ 1) for i in range(lax.axis_size("grp"))]
    packed = jnp.concatenate([x.reshape(frames, rows // frames, width) for x in (q, k, v)], axis=1)
    moved = all_to_all(packed)
    far_k = lax.ppermute(k, "grp", swap)
    far_v = lax.ppermute(v, "grp", swap)
    spatial = spatial_attention(clip_frames, clip_pixels, q, k, v, far_k, far_v, 0)
    moved, spatial = lax.optimization_barrier((moved, spatial))
    back = all_to_all(temporal_attention(clip_frames, moved, 6))
    attended = spatial + back.reshape(rows, width).astype(jnp.float32)
    return attended.astype(jnp.bfloat16)[None, None]


def solution(mesh):
    spec = P("grp", "seq", None, None)
    return jax.shard_map(
        on_device, mesh=mesh, in_specs=(spec, spec, spec, P(), P()), out_specs=spec, check_vma=False
    )
```

```python
import functools

import jax
import jax.numpy as jnp
from jax import lax
from jax.experimental import pallas as pl
from jax.experimental.pallas import tpu as pltpu
from jax.sharding import PartitionSpec as P

DH = 128
CLIPS = 4
MASKED = -1e30
SCALE = DH**-0.5 * 1.4426950408889634
TBLOCK = 16
SHIFTS = (7, 9, 6, 10, 5, 11, 8, 4, 12, 3, 13, 2, 14, 1, 15)
SLOTS = SHIFTS + (0,)
PARAMS = pltpu.CompilerParams(vmem_limit_bytes=24 * 1024 * 1024)
WIDE = pltpu.CompilerParams(vmem_limit_bytes=60 * 1024 * 1024)
SMEM = pl.BlockSpec(memory_space=pltpu.SMEM)


def scores_of(a, b):
    return lax.dot_general(a, b, (((1,), (1,)), ((), ())), preferred_element_type=jnp.float32)


def product(a, b):
    return jnp.dot(a, b, preferred_element_type=jnp.float32)


def spatial_kernel(cf_ref, cp_ref, q_ref, k_ref, v_ref, fk_ref, fv_ref, o_ref):
    group_slot = lax.axis_index("grp")
    frame = lax.axis_index("seq")
    group = group_slot // 2
    half = group_slot % 2
    rows = q_ref.shape[0]
    limit = cp_ref[group, 0]
    end = cf_ref[group, 0]
    for clip in range(1, CLIPS):
        limit = jnp.where(frame >= end, cp_ref[group, clip], limit)
        end = end + cf_ref[group, clip]
    column = lax.broadcasted_iota(jnp.int32, (1, rows), 1)
    own_keep = column < limit - half * rows
    far_keep = column < limit - (1 - half) * rows
    for head in range(q_ref.shape[1] // DH):
        lanes = pl.ds(head * DH, DH)
        q = q_ref[:, lanes]
        own = jnp.where(own_keep, scores_of(q, k_ref[:, lanes]), MASKED)
        far = jnp.where(far_keep, scores_of(q, fk_ref[:, lanes]), MASKED)
        top = jnp.maximum(
            jnp.max(own, axis=1, keepdims=True), jnp.max(far, axis=1, keepdims=True)
        )
        own = jnp.exp2((own - top) * SCALE)
        far = jnp.exp2((far - top) * SCALE)
        total = jnp.sum(own, axis=1, keepdims=True) + jnp.sum(far, axis=1, keepdims=True)
        summed = product(own.astype(jnp.bfloat16), v_ref[:, lanes])
        summed = summed + product(far.astype(jnp.bfloat16), fv_ref[:, lanes])
        o_ref[:, lanes] = summed / total


def spatial_attention(clip_frames, clip_pixels, q, k, v, far_k, far_v, start):
    rows, width = far_k.shape
    heads = width // DH
    block = pl.BlockSpec((rows, DH), lambda h: (0, h))
    whole = pl.BlockSpec((rows, DH), lambda h: (0, h + start // DH))
    return pl.pallas_call(
        spatial_kernel,
        grid=(heads,),
        in_specs=[SMEM, SMEM, whole, whole, whole, block, block],
        out_specs=block,
        out_shape=jax.ShapeDtypeStruct((rows, width), jnp.float32),
        compiler_params=PARAMS,
        cost_estimate=pl.CostEstimate(
            flops=8 * rows * rows * width,
            bytes_accessed=rows * width * 14,
            transcendentals=2 * rows * rows * heads,
        ),
        name="spatial",
    )(clip_frames, clip_pixels, q, k, v, far_k, far_v)


def came_from(slot, frames):
    return lax.rem(lax.axis_index("seq") + frames - slot, frames)


def clip_bias(cf_ref, frames):
    size = frames * TBLOCK
    group = lax.axis_index("grp") // 2

    def segment_of(frame):
        end = 0
        segment = jnp.zeros_like(frame)
        for clip in range(CLIPS):
            end = end + cf_ref[group, clip]
            segment = segment + (frame >= end).astype(jnp.int32)
        return segment

    row = lax.broadcasted_iota(jnp.int32, (size, 1), 0)
    col = lax.broadcasted_iota(jnp.int32, (1, size), 1)
    row_frame = jnp.zeros_like(row)
    for place, slot in enumerate(SLOTS):
        row_frame = jnp.where(row // TBLOCK == place, came_from(slot, frames), row_frame)
    same_spot = row % TBLOCK == col % TBLOCK
    same_clip = segment_of(row_frame) == segment_of(col // TBLOCK)
    return jnp.where(same_spot & same_clip, 0.0, MASKED)


def temporal_block(bias, q, k, v):
    scores = scores_of(q, k) + bias
    top = jnp.max(scores, axis=1, keepdims=True)
    weights = jnp.exp2((scores - top) * SCALE).astype(jnp.bfloat16)
    summed = product(weights, jnp.concatenate([v, jnp.ones_like(v)], axis=1))
    return (summed[:, :DH] / summed[:, DH:]).astype(jnp.bfloat16)


def temporal_kernel(cf_ref, qkv_ref, *refs):
    outs, bias_ref = refs[:-1], refs[-1]
    frames = len(outs)
    rows, width = outs[0].shape
    size = frames * TBLOCK

    @pl.when(pl.program_id(0) == 0)
    def _():
        bias_ref[...] = clip_bias(cf_ref, frames)

    bias = bias_ref[...]
    for head in range(width // DH):
        lanes = pl.ds(head * DH, DH)
        for block in range(rows // TBLOCK):
            at = pl.ds(block * TBLOCK, TBLOCK)
            q = jnp.concatenate(
                [qkv_ref[came_from(slot, frames), at, lanes] for slot in SLOTS], axis=0
            )
            k, v = (
                qkv_ref[:, pl.ds(which * rows + block * TBLOCK, TBLOCK), lanes].reshape(size, DH)
                for which in (1, 2)
            )
            out = temporal_block(bias, q, k, v)
            for place, o_ref in enumerate(outs):
                o_ref[at, lanes] = out[place * TBLOCK : (place + 1) * TBLOCK]


def temporal_cost(frames, rows, width):
    size = frames * TBLOCK
    return pl.CostEstimate(
        flops=4 * size * size * width * rows // TBLOCK,
        bytes_accessed=frames * rows * width * 8,
        transcendentals=size * size * (width // DH) * rows // TBLOCK,
    )


def temporal_attention(clip_frames, qkv, heads_step):
    frames, rows3, width = qkv.shape
    rows = rows3 // 3
    lanes = heads_step * DH
    size = frames * TBLOCK
    return pl.pallas_call(
        temporal_kernel,
        grid=(width // lanes,),
        in_specs=[SMEM, pl.BlockSpec((frames, rows3, lanes), lambda h: (0, 0, h))],
        out_specs=[pl.BlockSpec((rows, lanes), lambda h: (0, h))] * frames,
        out_shape=[jax.ShapeDtypeStruct((rows, width), jnp.bfloat16)] * frames,
        scratch_shapes=[pltpu.VMEM((size, size), jnp.float32)],
        compiler_params=WIDE,
        cost_estimate=temporal_cost(frames, rows, width),
        name="temporal",
    )(clip_frames, qkv)


def add_kernel(frames, spatial_ref, *refs):
    backs, o_ref = refs[:frames], refs[frames]
    share = backs[0].shape[0]
    for slot, back in zip(SLOTS, backs):
        start = lax.rem(lax.axis_index("seq") + slot, frames) * share
        at = pl.ds(pl.multiple_of(start, share), share)
        o_ref[at, :] = (spatial_ref[at, :] + back[...].astype(jnp.float32)).astype(o_ref.dtype)


def add_pieces(spatial, backs):
    rows, width = spatial.shape
    frames = len(backs)
    share = backs[0].shape[0]
    lanes = width // 2
    block = pl.BlockSpec((rows, lanes), lambda h: (0, h))
    return pl.pallas_call(
        functools.partial(add_kernel, frames),
        grid=(width // lanes,),
        in_specs=[block] + [pl.BlockSpec((share, lanes), lambda h: (0, h))] * frames,
        out_specs=block,
        out_shape=jax.ShapeDtypeStruct((rows, width), jnp.bfloat16),
        compiler_params=PARAMS,
        cost_estimate=pl.CostEstimate(
            flops=rows * width, bytes_accessed=8 * rows * width, transcendentals=0
        ),
        name="add_pieces",
    )(spatial, *backs)


def all_to_all(array):
    return lax.all_to_all(array, "seq", split_axis=0, concat_axis=0, tiled=True)


def on_device(queries, keys, values, clip_frames, clip_pixels):
    rows, width = queries.shape[2], queries.shape[3]
    frames = lax.axis_size("seq")
    q, k, v = queries[0, 0], keys[0, 0], values[0, 0]
    swap = [(i, i ^ 1) for i in range(lax.axis_size("grp"))]
    packed = jnp.concatenate([x.reshape(frames, rows // frames, width) for x in (q, k, v)], axis=1)
    moved = all_to_all(packed)
    far_k = lax.ppermute(k, "grp", swap)
    far_v = lax.ppermute(v, "grp", swap)
    spatial = spatial_attention(clip_frames, clip_pixels, q, k, v, far_k, far_v, 0)
    moved, spatial = lax.optimization_barrier((moved, spatial))
    outs = temporal_attention(clip_frames, moved, 6)
    backs = []
    for slot, out in zip(SLOTS, outs):
        pairs = [(i, (i + frames - slot) % frames) for i in range(frames)]
        backs.append(lax.ppermute(out, "seq", pairs) if slot else out)
    return add_pieces(spatial, backs)[None, None]


def solution(mesh):
    spec = P("grp", "seq", None, None)
    return jax.shard_map(
        on_device, mesh=mesh, in_specs=(spec, spec, spec, P(), P()), out_specs=spec, check_vma=False
    )
```

```python
import functools

import jax
import jax.numpy as jnp
from jax import lax
from jax.experimental import pallas as pl
from jax.experimental.pallas import tpu as pltpu
from jax.sharding import PartitionSpec as P

DH = 128
CLIPS = 4
MASKED = -1e30
SCALE = DH**-0.5 * 1.4426950408889634
TBLOCK = 16
SHIFTS = (7, 9, 6, 10, 5, 11, 8, 4, 12, 3, 13, 2, 14, 1, 15)
SLOTS = SHIFTS + (0,)
PARAMS = pltpu.CompilerParams(vmem_limit_bytes=24 * 1024 * 1024)
WIDE = pltpu.CompilerParams(vmem_limit_bytes=60 * 1024 * 1024)
SMEM = pl.BlockSpec(memory_space=pltpu.SMEM)


def scores_of(a, b):
    return lax.dot_general(a, b, (((1,), (1,)), ((), ())), preferred_element_type=jnp.float32)


def product(a, b):
    return jnp.dot(a, b, preferred_element_type=jnp.float32)


def spatial_kernel(cf_ref, cp_ref, q_ref, k_ref, v_ref, fk_ref, fv_ref, o_ref):
    group_slot = lax.axis_index("grp")
    frame = lax.axis_index("seq")
    group = group_slot // 2
    half = group_slot % 2
    rows = q_ref.shape[0]
    limit = cp_ref[group, 0]
    end = cf_ref[group, 0]
    for clip in range(1, CLIPS):
        limit = jnp.where(frame >= end, cp_ref[group, clip], limit)
        end = end + cf_ref[group, clip]
    column = lax.broadcasted_iota(jnp.int32, (1, rows), 1)
    own_keep = column < limit - half * rows
    far_keep = column < limit - (1 - half) * rows
    for head in range(q_ref.shape[1] // DH):
        lanes = pl.ds(head * DH, DH)
        q = q_ref[:, lanes]
        own = jnp.where(own_keep, scores_of(q, k_ref[:, lanes]), MASKED)
        far = jnp.where(far_keep, scores_of(q, fk_ref[:, lanes]), MASKED)
        top = jnp.maximum(
            jnp.max(own, axis=1, keepdims=True), jnp.max(far, axis=1, keepdims=True)
        )
        own = jnp.exp2((own - top) * SCALE)
        far = jnp.exp2((far - top) * SCALE)
        total = jnp.sum(own, axis=1, keepdims=True) + jnp.sum(far, axis=1, keepdims=True)
        summed = product(own.astype(jnp.bfloat16), v_ref[:, lanes])
        summed = summed + product(far.astype(jnp.bfloat16), fv_ref[:, lanes])
        o_ref[:, lanes] = (summed / total).astype(o_ref.dtype)


def spatial_attention(clip_frames, clip_pixels, q, k, v, far_k, far_v, start):
    rows, width = far_k.shape
    heads = width // DH
    block = pl.BlockSpec((rows, DH), lambda h: (0, h))
    whole = pl.BlockSpec((rows, DH), lambda h: (0, h + start // DH))
    return pl.pallas_call(
        spatial_kernel,
        grid=(heads,),
        in_specs=[SMEM, SMEM, whole, whole, whole, block, block],
        out_specs=block,
        out_shape=jax.ShapeDtypeStruct((rows, width), jnp.bfloat16),
        compiler_params=PARAMS,
        cost_estimate=pl.CostEstimate(
            flops=8 * rows * rows * width,
            bytes_accessed=rows * width * 14,
            transcendentals=2 * rows * rows * heads,
        ),
        name="spatial",
    )(clip_frames, clip_pixels, q, k, v, far_k, far_v)


def came_from(slot, frames):
    return lax.rem(lax.axis_index("seq") + frames - slot, frames)


def clip_bias(cf_ref, frames):
    size = frames * TBLOCK
    group = lax.axis_index("grp") // 2

    def segment_of(frame):
        end = 0
        segment = jnp.zeros_like(frame)
        for clip in range(CLIPS):
            end = end + cf_ref[group, clip]
            segment = segment + (frame >= end).astype(jnp.int32)
        return segment

    row = lax.broadcasted_iota(jnp.int32, (size, 1), 0)
    col = lax.broadcasted_iota(jnp.int32, (1, size), 1)
    row_frame = jnp.zeros_like(row)
    for place, slot in enumerate(SLOTS):
        row_frame = jnp.where(row // TBLOCK == place, came_from(slot, frames), row_frame)
    same_spot = row % TBLOCK == col % TBLOCK
    same_clip = segment_of(row_frame) == segment_of(col // TBLOCK)
    return jnp.where(same_spot & same_clip, 0.0, MASKED)


def temporal_block(bias, q, k, v):
    scores = scores_of(q, k) + bias
    top = jnp.max(scores, axis=1, keepdims=True)
    weights = jnp.exp2((scores - top) * SCALE).astype(jnp.bfloat16)
    summed = product(weights, jnp.concatenate([v, jnp.ones_like(v)], axis=1))
    return (summed[:, :DH] / summed[:, DH:]).astype(jnp.bfloat16)


def temporal_kernel(cf_ref, qkv_ref, *refs):
    outs, bias_ref = refs[:-1], refs[-1]
    frames = len(outs)
    rows, width = outs[0].shape
    size = frames * TBLOCK

    @pl.when(pl.program_id(0) == 0)
    def _():
        bias_ref[...] = clip_bias(cf_ref, frames)

    bias = bias_ref[...]
    for head in range(width // DH):
        lanes = pl.ds(head * DH, DH)
        for block in range(rows // TBLOCK):
            at = pl.ds(block * TBLOCK, TBLOCK)
            q = jnp.concatenate(
                [qkv_ref[came_from(slot, frames), at, lanes] for slot in SLOTS], axis=0
            )
            k, v = (
                qkv_ref[:, pl.ds(which * rows + block * TBLOCK, TBLOCK), lanes].reshape(size, DH)
                for which in (1, 2)
            )
            out = temporal_block(bias, q, k, v)
            for place, o_ref in enumerate(outs):
                o_ref[at, lanes] = out[place * TBLOCK : (place + 1) * TBLOCK]


def temporal_cost(frames, rows, width):
    size = frames * TBLOCK
    return pl.CostEstimate(
        flops=4 * size * size * width * rows // TBLOCK,
        bytes_accessed=frames * rows * width * 8,
        transcendentals=size * size * (width // DH) * rows // TBLOCK,
    )


def temporal_attention(clip_frames, qkv, heads_step):
    frames, rows3, width = qkv.shape
    rows = rows3 // 3
    lanes = heads_step * DH
    size = frames * TBLOCK
    return pl.pallas_call(
        temporal_kernel,
        grid=(width // lanes,),
        in_specs=[SMEM, pl.BlockSpec((frames, rows3, lanes), lambda h: (0, 0, h))],
        out_specs=[pl.BlockSpec((rows, lanes), lambda h: (0, h))] * frames,
        out_shape=[jax.ShapeDtypeStruct((rows, width), jnp.bfloat16)] * frames,
        scratch_shapes=[pltpu.VMEM((size, size), jnp.float32)],
        compiler_params=WIDE,
        cost_estimate=temporal_cost(frames, rows, width),
        name="temporal",
    )(clip_frames, qkv)


def add_kernel(frames, spatial_ref, *refs):
    backs, o_ref = refs[:frames], refs[frames]
    share = backs[0].shape[0]
    for slot, back in zip(SLOTS, backs):
        start = lax.rem(lax.axis_index("seq") + slot, frames) * share
        at = pl.ds(pl.multiple_of(start, share), share)
        both = spatial_ref[at, :].astype(jnp.float32) + back[...].astype(jnp.float32)
        o_ref[at, :] = both.astype(o_ref.dtype)


def add_pieces(spatial, backs):
    rows, width = spatial.shape
    frames = len(backs)
    share = backs[0].shape[0]
    lanes = width // 2
    block = pl.BlockSpec((rows, lanes), lambda h: (0, h))
    return pl.pallas_call(
        functools.partial(add_kernel, frames),
        grid=(width // lanes,),
        in_specs=[block] + [pl.BlockSpec((share, lanes), lambda h: (0, h))] * frames,
        out_specs=block,
        out_shape=jax.ShapeDtypeStruct((rows, width), jnp.bfloat16),
        compiler_params=PARAMS,
        cost_estimate=pl.CostEstimate(
            flops=rows * width, bytes_accessed=8 * rows * width, transcendentals=0
        ),
        name="add_pieces",
    )(spatial, *backs)


def all_to_all(array):
    return lax.all_to_all(array, "seq", split_axis=0, concat_axis=0, tiled=True)


def on_device(queries, keys, values, clip_frames, clip_pixels):
    rows, width = queries.shape[2], queries.shape[3]
    frames = lax.axis_size("seq")
    q, k, v = queries[0, 0], keys[0, 0], values[0, 0]
    swap = [(i, i ^ 1) for i in range(lax.axis_size("grp"))]
    packed = jnp.concatenate([x.reshape(frames, rows // frames, width) for x in (q, k, v)], axis=1)
    moved = all_to_all(packed)
    far_k = lax.ppermute(k, "grp", swap)
    far_v = lax.ppermute(v, "grp", swap)
    spatial = spatial_attention(clip_frames, clip_pixels, q, k, v, far_k, far_v, 0)
    moved, spatial = lax.optimization_barrier((moved, spatial))
    outs = temporal_attention(clip_frames, moved, 6)
    backs = []
    for slot, out in zip(SLOTS, outs):
        pairs = [(i, (i + frames - slot) % frames) for i in range(frames)]
        backs.append(lax.ppermute(out, "seq", pairs) if slot else out)
    return add_pieces(spatial, backs)[None, None]


def solution(mesh):
    spec = P("grp", "seq", None, None)
    return jax.shard_map(
        on_device, mesh=mesh, in_specs=(spec, spec, spec, P(), P()), out_specs=spec, check_vma=False
    )
```
